512 devices in a mesh: wide: 64 (over y, x, core), narrow: 8 (over z).
Axes of the slice: x: 4, y: 8, z: 8, core: 2. Of those that a mesh axis runs over, the one named last changes fastest.
Arguments:
- queries: bfloat16 [65536, 2048], P(('wide', 'narrow')), may hold values from -6 to 6
- keys: bfloat16 [65536, 2048], P(('wide', 'narrow')), may hold values from -6 to 6
- values: bfloat16 [65536, 2048], P(('wide', 'narrow')), may hold values from -6 to 6
- norm_gain: float32 [2048], replicated, may hold values from 0.1 to 1.9
Outputs:
- attended: bfloat16 [65536, 2048], P(('wide', 'narrow'))
The draws below stay inside these ranges and needn't reach their ends.
All inputs are finite; a program needn't handle non-finite values.
Results may differ from the reference program's by a relative error of at most 0.0032.
Values sent between devices are 32-bit elements; how exact they have to be, the bound alone decides.
No kernel may reach another device: no remote copies, remote signals or barrier semaphores. Data moves between devices by JAX's collectives and lax.ppermute only.
A program may use at most 192 MiB of HBM per device.

```python
import jax
import jax.numpy as jnp
from jax import lax

H = 16
DK = 128
TOK_DEV = 128
TOKENS = 65536


def levels(key, dims, pieces, smallest, high):
    def one(position, blocks):
        draws = jax.random.uniform(jax.random.fold_in(jax.random.fold_in(key, 6), position), (blocks,), jnp.float32, smallest / len(pieces), high / len(pieces))
        return jnp.repeat(jnp.exp(draws), dims[position] // blocks).reshape((-1,) + (1,) * (len(dims) - position - 1))

    loudness = one(*pieces[0])
    for cut in pieces[1:]:
        loudness = loudness * one(*cut)
    return loudness


def bell_draw(stream_key, extent, spread, limit, shards=(), dtype=jnp.bfloat16):
    array = spread * jax.random.normal(stream_key, extent, jnp.float32)
    if shards:
        array = array * levels(stream_key, extent, shards, -0.22, 0.18)
    return jnp.clip(array, -limit, limit).astype(dtype)


def setup_inputs(seed: int = 0) -> dict:
    arg_keys = jax.random.split(jax.random.key(seed), 5)
    queries = bell_draw(arg_keys[0], (TOKENS, H * DK), 1.0, 6.0, ((0, 512),))
    keys = bell_draw(arg_keys[1], (TOKENS, H * DK), 1.0, 6.0, ((0, 512),))
    values = bell_draw(arg_keys[2], (TOKENS, H * DK), 1.0, 6.0, ((0, 512),))
    norm_gain = jnp.clip(1.0 + 0.18 * jax.random.normal(arg_keys[3], (H * DK,), jnp.float32), 0.1, 1.9)
    return dict(queries=queries, keys=keys, values=values, norm_gain=norm_gain)


def reference(queries, keys, values, norm_gain):
    blocks = TOKENS // TOK_DEV
    feature_queries = (jax.nn.elu(queries.astype(jnp.float32)) + 1.0).astype(jnp.bfloat16)
    feature_keys = (jax.nn.elu(keys.astype(jnp.float32)) + 1.0).astype(jnp.bfloat16)
    feature_queries = feature_queries.reshape(blocks, TOK_DEV, H, DK)
    feature_keys = feature_keys.reshape(blocks, TOK_DEV, H, DK)
    value_rows = values.reshape(blocks, TOK_DEV, H, DK)
    causal = jnp.tril(jnp.ones((TOK_DEV, TOK_DEV), jnp.float32))
    gain = norm_gain.reshape(H, DK)

    def advance(kv_summary_state, item):
        query_tile, key_tile, value_tile = item
        scores = jnp.einsum('qhk,shk->hqs', query_tile.astype(jnp.float32), key_tile.astype(jnp.float32))
        weights = (scores * causal[None]).astype(jnp.bfloat16)
        inner = jnp.einsum('hqs,shv->qhv', weights.astype(jnp.float32), value_tile.astype(jnp.float32))
        outer_product = jnp.einsum('dtu,tuj->dtj', query_tile.astype(jnp.float32), kv_summary_state, precision=lax.Precision.HIGHEST)
        mixed = inner + outer_product
        meansq = lax.optimization_barrier(jnp.mean(mixed * mixed, axis=-1, keepdims=True))
        result = (gain[None] * mixed * lax.rsqrt(meansq + 1e-05)).astype(jnp.bfloat16)
        local_state = jnp.einsum('may,mai->ayi', key_tile.astype(jnp.float32), value_tile.astype(jnp.float32))
        return (kv_summary_state + local_state, result)
    start = jnp.zeros((H, DK, DK), jnp.float32)
    final_state, outputs = lax.scan(advance, start, (feature_queries, feature_keys, value_rows))
    return outputs.reshape(TOKENS, H * DK)
```

```python
import jax
import jax.numpy as jnp
from jax import lax
from jax.experimental import pallas as pl
from jax.experimental.pallas import tpu as pltpu
from jax.sharding import Mesh, PartitionSpec as P

H = 16
DK = 128
GROUP = ("x", "core", "z")
WHOLE = ("y", "x", "core", "z")
SIZES = (8, 4, 2, 8)


def feature(rows):
    wide = rows.astype(jnp.float32)
    grown = jnp.where(wide > 0.0, wide + 1.0, jnp.exp(jnp.minimum(wide, 0.0)))
    return grown.astype(jnp.bfloat16)


def state_kernel(keys_ref, values_ref, state_ref):
    for head in range(H):
        lanes = slice(head * DK, (head + 1) * DK)
        state_ref[head] = lax.dot_general(
            feature(keys_ref[:, lanes]),
            values_ref[:, lanes],
            (((0,), (0,)), ((), ())),
            preferred_element_type=jnp.float32,
        )


def scan_kernel(start_ref, parts_ref, prefix_ref):
    running = start_ref[...]
    for block in range(parts_ref.shape[0]):
        prefix_ref[block] = running
        running = running + parts_ref[block]


def attend_kernel(queries_ref, keys_ref, values_ref, gain_ref, prefix_ref, out_ref):
    rows = queries_ref.shape[0]
    at = lax.broadcasted_iota(jnp.int32, (rows, rows), 0)
    seen = lax.broadcasted_iota(jnp.int32, (rows, rows), 1)
    causal = seen <= at
    for head in range(H):
        lanes = slice(head * DK, (head + 1) * DK)
        fq = feature(queries_ref[:, lanes])
        fk = feature(keys_ref[:, lanes])
        scores = lax.dot_general(
            fq, fk, (((1,), (1,)), ((), ())), preferred_element_type=jnp.float32
        )
        weights = jnp.where(causal, scores, 0.0).astype(jnp.bfloat16)
        prefix = prefix_ref[head]
        high = prefix.astype(jnp.bfloat16)
        rest = prefix - high.astype(jnp.float32)
        middle = rest.astype(jnp.bfloat16)
        low = (rest - middle.astype(jnp.float32)).astype(jnp.bfloat16)
        left = jnp.concatenate([weights, fq, fq, fq], axis=1)
        right = jnp.concatenate([values_ref[:, lanes], high, middle, low], axis=0)
        mixed = jnp.dot(left, right, preferred_element_type=jnp.float32)
        meansq = jnp.mean(mixed * mixed, axis=-1, keepdims=True)
        scaled = gain_ref[:, lanes] * mixed * lax.rsqrt(meansq + 1e-05)
        out_ref[:, lanes] = scaled.astype(jnp.bfloat16)


def on_chip(kernel, shape, dtype, count):
    whole = pl.BlockSpec(memory_space=pltpu.VMEM)
    return pl.pallas_call(
        kernel,
        out_shape=jax.ShapeDtypeStruct(shape, dtype),
        in_specs=[whole] * count,
        out_specs=whole,
        compiler_params=pltpu.CompilerParams(vmem_limit_bytes=32 * 2**20),
    )


def local(queries, keys, values, norm_gain):
    rows = queries.shape[0]
    group = SIZES[1] * SIZES[2] * SIZES[3]
    piece = H * DK // group
    state = on_chip(state_kernel, (H, DK, DK), jnp.float32, 2)(keys, values)
    parts = lax.all_to_all(state.reshape(group, piece, DK), GROUP, 0, 0, tiled=True)
    total = jnp.sum(parts, axis=0)
    planes = lax.all_to_all(
        jnp.broadcast_to(total[None], (SIZES[0], piece, DK)), "y", 0, 0, tiled=True
    )
    before = jnp.arange(SIZES[0]) < lax.axis_index("y")
    start = jnp.sum(jnp.where(before[:, None, None], planes, 0.0), axis=0)
    prefix = on_chip(scan_kernel, parts.shape, jnp.float32, 2)(start, parts)
    prefix = lax.all_to_all(prefix, GROUP, 0, 0, tiled=True).reshape(H, DK, DK)
    return on_chip(attend_kernel, (rows, H * DK), jnp.bfloat16, 5)(
        queries, keys, values, norm_gain.reshape(1, H * DK), prefix
    )


def solution(mesh):
    mesh = Mesh(mesh.devices.reshape(SIZES), WHOLE)
    split = P(WHOLE, None)
    return jax.shard_map(
        local, mesh=mesh, in_specs=(split, split, split, P()), out_specs=split, check_vma=False
    )
```

```python
import itertools

import jax
import jax.numpy as jnp
from jax import lax
from jax.experimental import pallas as pl
from jax.experimental.pallas import tpu as pltpu
from jax.sharding import Mesh, PartitionSpec as P

H = 16
DK = 128
SIZES = (8, 4, 2, 8)
WHOLE = ("y", "x", "core", "z")
PLANE = ("z", "core", "x")
TOGETHER = 8
LOADS = 1
LIMIT = 16 * 2**20


def feature(rows):
    wide = rows.astype(jnp.float32)
    grown = jnp.where(wide > 0.0, wide + 1.0, jnp.exp(jnp.minimum(wide, 0.0)))
    return grown.astype(jnp.bfloat16)


def lanes_of(head):
    return slice(head * DK, (head + 1) * DK)


def state_kernel(keys_hbm, values_hbm, state_ref, keys_ref, values_ref, arrived):
    loads = []
    for number, (source, target) in enumerate(
        ((keys_hbm, keys_ref), (values_hbm, values_ref))
    ):
        for half in range(LOADS):
            rows = pl.ds(half * (target.shape[0] // LOADS), target.shape[0] // LOADS)
            load = pltpu.make_async_copy(
                source.at[rows], target.at[rows], arrived.at[number, half]
            )
            load.start()
            loads.append(load)
    for load in loads:
        load.wait()
    for head in range(H):
        state_ref[head] = lax.dot_general(
            feature(keys_ref[:, lanes_of(head)]),
            values_ref[:, lanes_of(head)],
            (((0,), (0,)), ((), ())),
            preferred_element_type=jnp.float32,
        )


def total_kernel(parts_ref, totals_ref):
    sums = [parts_ref[lane] for lane in range(4)]
    for block in range(4, parts_ref.shape[0]):
        sums[block % 4] = sums[block % 4] + parts_ref[block]
    total = (sums[0] + sums[1]) + (sums[2] + sums[3])
    for plane in range(totals_ref.shape[0]):
        totals_ref[plane] = total


def scan_kernel(planes_ref, parts_ref, prefix_ref):
    place = lax.axis_index("y")
    running = jnp.zeros_like(planes_ref[0])
    for plane in range(planes_ref.shape[0] - 1):
        running = running + jnp.where(plane < place, planes_ref[plane], 0.0)
    for x, core, z in itertools.product(*(range(size) for size in SIZES[1:])):
        block = (z * SIZES[2] + core) * SIZES[1] + x
        prefix_ref[block] = running
        running = running + parts_ref[block]


def attend_kernel(queries_ref, keys_ref, values_ref, gain_ref, prefix_ref, out_ref):
    rows = queries_ref.shape[0]
    at = lax.broadcasted_iota(jnp.int32, (rows, rows), 0)
    seen = lax.broadcasted_iota(jnp.int32, (rows, rows), 1)
    causal = seen <= at
    for first in range(0, H, TOGETHER):
        heads = range(first, first + TOGETHER)
        fq = [feature(queries_ref[:, lanes_of(head)]) for head in heads]
        fk = [feature(keys_ref[:, lanes_of(head)]) for head in heads]
        scores = [
            lax.dot_general(a, b, (((1,), (1,)), ((), ())), preferred_element_type=jnp.float32)
            for a, b in zip(fq, fk)
        ]
        weights = [jnp.where(causal, part, 0.0).astype(jnp.bfloat16) for part in scores]
        mixed = []
        for head, a, w in zip(heads, fq, weights):
            prefix = prefix_ref[head]
            high = prefix.astype(jnp.bfloat16)
            rest = prefix - high.astype(jnp.float32)
            middle = rest.astype(jnp.bfloat16)
            low = (rest - middle.astype(jnp.float32)).astype(jnp.bfloat16)
            mixed.append(
                jnp.dot(
                    jnp.concatenate([w, a, a, a], axis=1),
                    jnp.concatenate([values_ref[:, lanes_of(head)], high, middle, low], axis=0),
                    preferred_element_type=jnp.float32,
                )
            )
        for head, part in zip(heads, mixed):
            meansq = jnp.mean(part * part, axis=-1, keepdims=True)
            scaled = gain_ref[:, lanes_of(head)] * part * lax.rsqrt(meansq + 1e-05)
            out_ref[:, lanes_of(head)] = scaled.astype(jnp.bfloat16)


def on_chip(kernel, count, *results, flops=0):
    whole = pl.BlockSpec(memory_space=pltpu.VMEM)
    shapes = [jax.ShapeDtypeStruct(shape, dtype) for shape, dtype in results]
    return pl.pallas_call(
        kernel,
        out_shape=shapes,
        in_specs=[whole] * count,
        out_specs=[whole] * len(shapes),
        compiler_params=pltpu.CompilerParams(vmem_limit_bytes=12 * 2**20),
        cost_estimate=pl.CostEstimate(
            flops=flops, bytes_accessed=3 * 2**20, transcendentals=0
        ),
    )


def local(queries, keys, values, norm_gain):
    rows, width = queries.shape
    planes, group = SIZES[0], SIZES[1] * SIZES[2] * SIZES[3]
    piece = width // group
    f32 = jnp.float32
    flops = 2 * H * rows * DK * DK
    state = pl.pallas_call(
        state_kernel,
        out_shape=jax.ShapeDtypeStruct((H, DK, DK), f32),
        in_specs=[pl.BlockSpec(memory_space=pl.ANY)] * 2,
        out_specs=pl.BlockSpec(memory_space=pltpu.VMEM),
        scratch_shapes=[pltpu.VMEM((rows, width), jnp.bfloat16)] * 2
        + [pltpu.SemaphoreType.DMA((2, LOADS))],
        compiler_params=pltpu.CompilerParams(vmem_limit_bytes=LIMIT),
    )(*(pltpu.with_memory_space_constraint(part, pltpu.HBM) for part in (keys, values)))
    parts = lax.all_to_all(state.reshape(group, piece, DK), PLANE, 0, 0, tiled=True)
    [totals] = on_chip(total_kernel, 1, ((planes, piece, DK), f32))(parts)
    totals = lax.all_to_all(totals, "y", 0, 0, tiled=True)
    [prefix] = on_chip(scan_kernel, 2, (parts.shape, f32))(totals, parts)
    prefix = lax.all_to_all(prefix, PLANE, 0, 0, tiled=True).reshape(H, DK, DK)
    [out] = on_chip(attend_kernel, 5, ((rows, width), jnp.bfloat16), flops=7 * flops)(
        queries, keys, values, norm_gain.reshape(1, width), prefix
    )
    return out


def solution(mesh):
    mesh = Mesh(mesh.devices.reshape(SIZES), WHOLE)
    split = P(WHOLE, None)
    return jax.shard_map(
        local, mesh=mesh, in_specs=(split, split, split, P()), out_specs=split, check_vma=False
    )
```

```python
import itertools

import jax
import jax.numpy as jnp
from jax import lax
from jax.experimental import pallas as pl
from jax.experimental.pallas import tpu as pltpu
from jax.sharding import Mesh, PartitionSpec as P

H = 16
DK = 128
SIZES = (8, 4, 2, 8)
WHOLE = ("y", "x", "core", "z")
PLANE = ("z", "core", "x")
TOGETHER = 8
LIMIT = 16 * 2**20


def feature(rows):
    wide = rows.astype(jnp.float32)
    grown = jnp.where(wide > 0.0, wide + 1.0, jnp.exp(jnp.minimum(wide, 0.0)))
    return grown.astype(jnp.bfloat16)


def lanes_of(head):
    return slice(head * DK, (head + 1) * DK)


def scores_of(fq, fk, causal):
    scores = lax.dot_general(
        fq, fk, (((1,), (1,)), ((), ())), preferred_element_type=jnp.float32
    )
    return jnp.where(causal, scores, 0.0).astype(jnp.bfloat16)


def mask_of(rows):
    at = lax.broadcasted_iota(jnp.int32, (rows, rows), 0)
    return lax.broadcasted_iota(jnp.int32, (rows, rows), 1) <= at


def in_three(prefix):
    high = prefix.astype(jnp.bfloat16)
    rest = prefix - high.astype(jnp.float32)
    middle = rest.astype(jnp.bfloat16)
    return [high, middle, (rest - middle.astype(jnp.float32)).astype(jnp.bfloat16)]


def normed(mixed, gain):
    meansq = jnp.mean(mixed * mixed, axis=-1, keepdims=True)
    return (gain * mixed * lax.rsqrt(meansq + 1e-05)).astype(jnp.bfloat16)


def waits_first():
    return lax.axis_index("z") < SIZES[3] // 2


def state_kernel(
    keys_hbm,
    values_hbm,
    queries_hbm,
    state_ref,
    inner_ref,
    features_ref,
    keys_ref,
    values_ref,
    queries_ref,
    arrived,
):
    loads = [
        pltpu.make_async_copy(source, target, arrived.at[number])
        for number, (source, target) in enumerate(
            (
                (keys_hbm, keys_ref),
                (values_hbm, values_ref),
                (queries_hbm, queries_ref),
            )
        )
    ]
    for load in loads[:2]:
        load.start()
    for load in loads[:2]:
        load.wait()
    for head in range(H):
        state_ref[head] = lax.dot_general(
            feature(keys_ref[:, lanes_of(head)]),
            values_ref[:, lanes_of(head)],
            (((0,), (0,)), ((), ())),
            preferred_element_type=jnp.float32,
        )
    @pl.when(waits_first())
    def _():
        loads[2].start()
        loads[2].wait()
        causal = mask_of(queries_ref.shape[0])
        for first in range(0, H, TOGETHER):
            lanes = [lanes_of(head) for head in range(first, first + TOGETHER)]
            fq = [feature(queries_ref[:, part]) for part in lanes]
            fk = [feature(keys_ref[:, part]) for part in lanes]
            weights = [scores_of(a, b, causal) for a, b in zip(fq, fk)]
            for part, a, w in zip(lanes, fq, weights):
                inner_ref[:, part] = jnp.dot(
                    w, values_ref[:, part], preferred_element_type=jnp.float32
                )
                features_ref[:, part] = a


def total_kernel(parts_ref, totals_ref):
    sums = [parts_ref[lane] for lane in range(4)]
    for block in range(4, parts_ref.shape[0]):
        sums[block % 4] = sums[block % 4] + parts_ref[block]
    total = (sums[0] + sums[1]) + (sums[2] + sums[3])
    for plane in range(totals_ref.shape[0]):
        totals_ref[plane] = total


def scan_kernel(planes_ref, parts_ref, prefix_ref):
    place = lax.axis_index("y")
    running = jnp.zeros_like(planes_ref[0])
    for plane in range(planes_ref.shape[0] - 1):
        running = running + jnp.where(plane < place, planes_ref[plane], 0.0)
    for x, core, z in itertools.product(*(range(size) for size in SIZES[1:])):
        block = (z * SIZES[2] + core) * SIZES[1] + x
        prefix_ref[block] = running
        running = running + parts_ref[block]


def attend_kernel(
    queries_ref,
    keys_ref,
    values_ref,
    gain_ref,
    prefix_ref,
    inner_ref,
    features_ref,
    out_hbm,
    out_ref,
    left,
):
    def store(first):
        done = pl.ds(first * DK, TOGETHER * DK)
        return pltpu.make_async_copy(
            out_ref.at[:, done], out_hbm.at[:, done], left.at[first // TOGETHER]
        )

    @pl.when(waits_first())
    def _():
        for first in range(0, H, TOGETHER):
            for head in range(first, first + TOGETHER):
                lanes = lanes_of(head)
                fq = features_ref[:, lanes]
                outer = jnp.dot(
                    jnp.concatenate([fq] * 3, axis=1),
                    jnp.concatenate(in_three(prefix_ref[head]), axis=0),
                    preferred_element_type=jnp.float32,
                )
                out_ref[:, lanes] = normed(inner_ref[:, lanes] + outer, gain_ref[:, lanes])
            store(first).start()

    @pl.when(jnp.logical_not(waits_first()))
    def _():
        causal = mask_of(queries_ref.shape[0])
        for first in range(0, H, TOGETHER):
            heads = range(first, first + TOGETHER)
            fq = [feature(queries_ref[:, lanes_of(head)]) for head in heads]
            fk = [feature(keys_ref[:, lanes_of(head)]) for head in heads]
            weights = [scores_of(a, b, causal) for a, b in zip(fq, fk)]
            mixed = []
            for head, a, w in zip(heads, fq, weights):
                right = [values_ref[:, lanes_of(head)], *in_three(prefix_ref[head])]
                mixed.append(
                    jnp.dot(
                        jnp.concatenate([w, a, a, a], axis=1),
                        jnp.concatenate(right, axis=0),
                        preferred_element_type=jnp.float32,
                    )
                )
            for head, part in zip(heads, mixed):
                out_ref[:, lanes_of(head)] = normed(part, gain_ref[:, lanes_of(head)])
            store(first).start()

    for first in range(0, H, TOGETHER):
        store(first).wait()


def on_chip(kernel, count, *results, flops=0):
    whole = pl.BlockSpec(memory_space=pltpu.VMEM)
    shapes = [jax.ShapeDtypeStruct(shape, dtype) for shape, dtype in results]
    return pl.pallas_call(
        kernel,
        out_shape=shapes,
        in_specs=[whole] * count,
        out_specs=[whole] * len(shapes),
        compiler_params=pltpu.CompilerParams(vmem_limit_bytes=12 * 2**20),
        cost_estimate=pl.CostEstimate(
            flops=flops, bytes_accessed=3 * 2**20, transcendentals=0
        ),
    )


def local(queries, keys, values, norm_gain):
    rows, width = queries.shape
    planes, group = SIZES[0], SIZES[1] * SIZES[2] * SIZES[3]
    piece = width // group
    f32 = jnp.float32
    flops = 2 * H * rows * DK * DK
    state, inner, features = pl.pallas_call(
        state_kernel,
        out_shape=[
            jax.ShapeDtypeStruct((H, DK, DK), f32),
            jax.ShapeDtypeStruct((rows, width), f32),
            jax.ShapeDtypeStruct((rows, width), jnp.bfloat16),
        ],
        in_specs=[pl.BlockSpec(memory_space=pl.ANY)] * 3,
        out_specs=[pl.BlockSpec(memory_space=pltpu.VMEM)] * 3,
        scratch_shapes=[pltpu.VMEM((rows, width), jnp.bfloat16)] * 3
        + [pltpu.SemaphoreType.DMA((3,))],
        compiler_params=pltpu.CompilerParams(vmem_limit_bytes=LIMIT),
    )(*(pltpu.with_memory_space_constraint(part, pltpu.HBM) for part in (keys, values, queries)))
    parts = lax.all_to_all(state.reshape(group, piece, DK), PLANE, 0, 0, tiled=True)
    [totals] = on_chip(total_kernel, 1, ((planes, piece, DK), f32))(parts)
    totals = lax.all_to_all(totals, "y", 0, 0, tiled=True)
    [prefix] = on_chip(scan_kernel, 2, (parts.shape, f32))(totals, parts)
    prefix = lax.all_to_all(prefix, PLANE, 0, 0, tiled=True).reshape(H, DK, DK)
    return pl.pallas_call(
        attend_kernel,
        out_shape=jax.ShapeDtypeStruct((rows, width), jnp.bfloat16),
        in_specs=[pl.BlockSpec(memory_space=pltpu.VMEM)] * 7,
        out_specs=pl.BlockSpec(memory_space=pl.ANY),
        scratch_shapes=[
            pltpu.VMEM((rows, width), jnp.bfloat16),
            pltpu.SemaphoreType.DMA((H // TOGETHER,)),
        ],
        compiler_params=pltpu.CompilerParams(vmem_limit_bytes=LIMIT),
    )(queries, keys, values, norm_gain.reshape(1, width), prefix, inner, features)


def solution(mesh):
    mesh = Mesh(mesh.devices.reshape(SIZES), WHOLE)
    split = P(WHOLE, None)
    return jax.shard_map(
        local, mesh=mesh, in_specs=(split, split, split, P()), out_specs=split, check_vma=False
    )
```

```python
import itertools

import jax
import jax.numpy as jnp
from jax import lax
from jax.experimental import pallas as pl
from jax.experimental.pallas import tpu as pltpu
from jax.sharding import Mesh, PartitionSpec as P

H = 16
DK = 128
SIZES = (8, 4, 2, 8)
BITS = {"y": ("y2", "y1", "y0"), "x": ("x1", "x0"), "core": ("core",), "z": ("z2", "z1", "z0")}
WHOLE = tuple(bit for axis in BITS.values() for bit in axis)
ROWS = ("y0", "y1", "y2")
PLANE = ("z2", "z1", "z0", "core", "x1", "x0")


def index_in(order, **place):
    index = 0
    for bit in order:
        axis = bit.rstrip("012")
        index = 2 * index + (place[axis] >> int(bit[len(axis) :] or 0)) % 2
    return index


TOGETHER = 8
LIMIT = 16 * 2**20


def feature(rows):
    wide = rows.astype(jnp.float32)
    grown = jnp.where(wide > 0.0, wide + 1.0, jnp.exp(jnp.minimum(wide, 0.0)))
    return grown.astype(jnp.bfloat16)


def lanes_of(head):
    return slice(head * DK, (head + 1) * DK)


def scores_of(fq, fk, causal):
    scores = lax.dot_general(
        fq, fk, (((1,), (1,)), ((), ())), preferred_element_type=jnp.float32
    )
    return jnp.where(causal, scores, 0.0).astype(jnp.bfloat16)


def mask_of(rows):
    at = lax.broadcasted_iota(jnp.int32, (rows, rows), 0)
    return lax.broadcasted_iota(jnp.int32, (rows, rows), 1) <= at


def in_three(prefix):
    high = prefix.astype(jnp.bfloat16)
    rest = prefix - high.astype(jnp.float32)
    middle = rest.astype(jnp.bfloat16)
    return [high, middle, (rest - middle.astype(jnp.float32)).astype(jnp.bfloat16)]


def normed(mixed, gain):
    meansq = jnp.mean(mixed * mixed, axis=-1, keepdims=True)
    return (gain * mixed * lax.rsqrt(meansq + 1e-05)).astype(jnp.bfloat16)


def waits_first():
    return lax.axis_index(BITS["z"]) < SIZES[3] // 2


def state_kernel(
    keys_hbm,
    values_hbm,
    queries_hbm,
    state_ref,
    inner_ref,
    features_ref,
    keys_ref,
    values_ref,
    queries_ref,
    arrived,
):
    loads = [
        pltpu.make_async_copy(source, target, arrived.at[number])
        for number, (source, target) in enumerate(
            (
                (keys_hbm, keys_ref),
                (values_hbm, values_ref),
                (queries_hbm, queries_ref),
            )
        )
    ]
    for load in loads[:2]:
        load.start()
    for load in loads[:2]:
        load.wait()
    for head in range(H):
        state_ref[head] = lax.dot_general(
            feature(keys_ref[:, lanes_of(head)]),
            values_ref[:, lanes_of(head)],
            (((0,), (0,)), ((), ())),
            preferred_element_type=jnp.float32,
        )
    @pl.when(waits_first())
    def _():
        loads[2].start()
        loads[2].wait()
        causal = mask_of(queries_ref.shape[0])
        for first in range(0, H, TOGETHER):
            lanes = [lanes_of(head) for head in range(first, first + TOGETHER)]
            fq = [feature(queries_ref[:, part]) for part in lanes]
            fk = [feature(keys_ref[:, part]) for part in lanes]
            weights = [scores_of(a, b, causal) for a, b in zip(fq, fk)]
            for part, a, w in zip(lanes, fq, weights):
                inner_ref[:, part] = jnp.dot(
                    w, values_ref[:, part], preferred_element_type=jnp.float32
                )
                features_ref[:, part] = a


def total_kernel(parts_ref, totals_ref):
    sums = [parts_ref[lane] for lane in range(4)]
    for block in range(4, parts_ref.shape[0]):
        sums[block % 4] = sums[block % 4] + parts_ref[block]
    total = (sums[0] + sums[1]) + (sums[2] + sums[3])
    for plane in range(totals_ref.shape[0]):
        totals_ref[plane] = total


def scan_kernel(planes_ref, parts_ref, prefix_ref):
    place = lax.axis_index(BITS["y"])
    running = jnp.zeros_like(planes_ref[0])
    for plane in range(planes_ref.shape[0] - 1):
        running = running + jnp.where(plane < place, planes_ref[index_in(ROWS, y=plane)], 0.0)
    for x, core, z in itertools.product(*(range(size) for size in SIZES[1:])):
        block = index_in(PLANE, x=x, core=core, z=z)
        prefix_ref[block] = running
        running = running + parts_ref[block]


def attend_kernel(
    queries_ref,
    keys_ref,
    values_ref,
    gain_ref,
    prefix_ref,
    inner_ref,
    features_ref,
    out_hbm,
    out_ref,
    left,
):
    def store(first):
        done = pl.ds(first * DK, TOGETHER * DK)
        return pltpu.make_async_copy(
            out_ref.at[:, done], out_hbm.at[:, done], left.at[first // TOGETHER]
        )

    @pl.when(waits_first())
    def _():
        for first in range(0, H, TOGETHER):
            for head in range(first, first + TOGETHER):
                lanes = lanes_of(head)
                fq = features_ref[:, lanes]
                outer = jnp.dot(
                    jnp.concatenate([fq] * 3, axis=1),
                    jnp.concatenate(in_three(prefix_ref[head]), axis=0),
                    preferred_element_type=jnp.float32,
                )
                out_ref[:, lanes] = normed(inner_ref[:, lanes] + outer, gain_ref[:, lanes])
            store(first).start()

    @pl.when(jnp.logical_not(waits_first()))
    def _():
        causal = mask_of(queries_ref.shape[0])
        for first in range(0, H, TOGETHER):
            heads = range(first, first + TOGETHER)
            fq = [feature(queries_ref[:, lanes_of(head)]) for head in heads]
            fk = [feature(keys_ref[:, lanes_of(head)]) for head in heads]
            weights = [scores_of(a, b, causal) for a, b in zip(fq, fk)]
            mixed = []
            for head, a, w in zip(heads, fq, weights):
                right = [values_ref[:, lanes_of(head)], *in_three(prefix_ref[head])]
                mixed.append(
                    jnp.dot(
                        jnp.concatenate([w, a, a, a], axis=1),
                        jnp.concatenate(right, axis=0),
                        preferred_element_type=jnp.float32,
                    )
                )
            for head, part in zip(heads, mixed):
                out_ref[:, lanes_of(head)] = normed(part, gain_ref[:, lanes_of(head)])
            store(first).start()

    for first in range(0, H, TOGETHER):
        store(first).wait()


def on_chip(kernel, count, *results, flops=0):
    whole = pl.BlockSpec(memory_space=pltpu.VMEM)
    shapes = [jax.ShapeDtypeStruct(shape, dtype) for shape, dtype in results]
    return pl.pallas_call(
        kernel,
        out_shape=shapes,
        in_specs=[whole] * count,
        out_specs=[whole] * len(shapes),
        compiler_params=pltpu.CompilerParams(vmem_limit_bytes=12 * 2**20),
        cost_estimate=pl.CostEstimate(
            flops=flops, bytes_accessed=3 * 2**20, transcendentals=0
        ),
    )


def local(queries, keys, values, norm_gain):
    rows, width = queries.shape
    planes, group = SIZES[0], SIZES[1] * SIZES[2] * SIZES[3]
    piece = width // group
    f32 = jnp.float32
    flops = 2 * H * rows * DK * DK
    state, inner, features = pl.pallas_call(
        state_kernel,
        out_shape=[
            jax.ShapeDtypeStruct((H, DK, DK), f32),
            jax.ShapeDtypeStruct((rows, width), f32),
            jax.ShapeDtypeStruct((rows, width), jnp.bfloat16),
        ],
        in_specs=[pl.BlockSpec(memory_space=pl.ANY)] * 3,
        out_specs=[pl.BlockSpec(memory_space=pltpu.VMEM)] * 3,
        scratch_shapes=[pltpu.VMEM((rows, width), jnp.bfloat16)] * 3
        + [pltpu.SemaphoreType.DMA((3,))],
        compiler_params=pltpu.CompilerParams(vmem_limit_bytes=LIMIT),
    )(*(pltpu.with_memory_space_constraint(part, pltpu.HBM) for part in (keys, values, queries)))
    parts = lax.all_to_all(state.reshape(group, piece, DK), PLANE, 0, 0, tiled=True)
    [totals] = on_chip(total_kernel, 1, ((planes, piece, DK), f32))(parts)
    totals = lax.all_to_all(totals, ROWS, 0, 0, tiled=True)
    [prefix] = on_chip(scan_kernel, 2, (parts.shape, f32))(totals, parts)
    prefix = lax.all_to_all(prefix, PLANE, 0, 0, tiled=True).reshape(H, DK, DK)
    return pl.pallas_call(
        attend_kernel,
        out_shape=jax.ShapeDtypeStruct((rows, width), jnp.bfloat16),
        in_specs=[pl.BlockSpec(memory_space=pltpu.VMEM)] * 7,
        out_specs=pl.BlockSpec(memory_space=pl.ANY),
        scratch_shapes=[
            pltpu.VMEM((rows, width), jnp.bfloat16),
            pltpu.SemaphoreType.DMA((H // TOGETHER,)),
        ],
        compiler_params=pltpu.CompilerParams(vmem_limit_bytes=LIMIT),
    )(queries, keys, values, norm_gain.reshape(1, width), prefix, inner, features)


def solution(mesh):
    mesh = Mesh(mesh.devices.reshape((2,) * len(WHOLE)), WHOLE)
    split = P(WHOLE, None)
    return jax.shard_map(
        local, mesh=mesh, in_specs=(split, split, split, P()), out_specs=split, check_vma=False
    )
```

```python
import itertools

import jax
import jax.numpy as jnp
from jax import lax
from jax.experimental import pallas as pl
from jax.experimental.pallas import tpu as pltpu
from jax.sharding import Mesh, PartitionSpec as P

H = 16
DK = 128
SIZES = (8, 4, 2, 8)
BITS = {"y": ("y2", "y1", "y0"), "x": ("x1", "x0"), "core": ("core",), "z": ("z2", "z1", "z0")}
WHOLE = tuple(bit for axis in BITS.values() for bit in axis)
ROWS = ("y0", "y1", "y2")
PLANE = ("z2", "z1", "z0", "core", "x1", "x0")


def index_in(order, **place):
    index = 0
    for bit in order:
        axis = bit.rstrip("012")
        index = 2 * index + (place[axis] >> int(bit[len(axis) :] or 0)) % 2
    return index


TOGETHER = 8
LIMIT = 16 * 2**20


def feature(rows):
    wide = rows.astype(jnp.float32)
    grown = jnp.where(wide > 0.0, wide + 1.0, jnp.exp(jnp.minimum(wide, 0.0)))
    return grown.astype(jnp.bfloat16)


def lanes_of(head):
    return slice(head * DK, (head + 1) * DK)


def scores_of(fq, fk, causal):
    scores = lax.dot_general(
        fq, fk, (((1,), (1,)), ((), ())), preferred_element_type=jnp.float32
    )
    return jnp.where(causal, scores, 0.0).astype(jnp.bfloat16)


def mask_of(rows):
    at = lax.broadcasted_iota(jnp.int32, (rows, rows), 0)
    return lax.broadcasted_iota(jnp.int32, (rows, rows), 1) <= at


def in_three(prefix):
    high = prefix.astype(jnp.bfloat16)
    rest = prefix - high.astype(jnp.float32)
    middle = rest.astype(jnp.bfloat16)
    return [high, middle, (rest - middle.astype(jnp.float32)).astype(jnp.bfloat16)]


def normed(mixed, gain):
    meansq = jnp.mean(mixed * mixed, axis=-1, keepdims=True)
    return (gain * mixed * lax.rsqrt(meansq + 1e-05)).astype(jnp.bfloat16)


def waits_first():
    return lax.axis_index(BITS["z"]) < SIZES[3] // 2


def state_kernel(
    keys_hbm,
    values_hbm,
    queries_hbm,
    state_ref,
    inner_ref,
    features_ref,
    keys_ref,
    values_ref,
    queries_ref,
    arrived,
):
    def load(number, half):
        source, target = (
            (keys_hbm, keys_ref),
            (values_hbm, values_ref),
            (queries_hbm, queries_ref),
        )[number]
        rows = pl.ds(half * (target.shape[0] // 2), target.shape[0] // 2)
        return pltpu.make_async_copy(
            source.at[rows], target.at[rows], arrived.at[number, half]
        )

    for half in range(2):
        for number in range(2):
            load(number, half).start()
    for half in range(2):
        rows = slice(half * (keys_ref.shape[0] // 2), (half + 1) * (keys_ref.shape[0] // 2))
        for number in range(2):
            load(number, half).wait()
        for head in range(H):
            part = lax.dot_general(
                feature(keys_ref[rows, lanes_of(head)]),
                values_ref[rows, lanes_of(head)],
                (((0,), (0,)), ((), ())),
                preferred_element_type=jnp.float32,
            )
            state_ref[head] = part if half == 0 else state_ref[head] + part

    @pl.when(waits_first())
    def _():
        for half in range(2):
            load(2, half).start()
        for half in range(2):
            load(2, half).wait()
        causal = mask_of(queries_ref.shape[0])
        for first in range(0, H, TOGETHER):
            lanes = [lanes_of(head) for head in range(first, first + TOGETHER)]
            fq = [feature(queries_ref[:, part]) for part in lanes]
            fk = [feature(keys_ref[:, part]) for part in lanes]
            weights = [scores_of(a, b, causal) for a, b in zip(fq, fk)]
            for part, a, w in zip(lanes, fq, weights):
                inner_ref[:, part] = jnp.dot(
                    w, values_ref[:, part], preferred_element_type=jnp.float32
                )
                features_ref[:, part] = a


def total_kernel(parts_ref, totals_ref):
    sums = [parts_ref[lane] for lane in range(4)]
    for block in range(4, parts_ref.shape[0]):
        sums[block % 4] = sums[block % 4] + parts_ref[block]
    total = (sums[0] + sums[1]) + (sums[2] + sums[3])
    for plane in range(totals_ref.shape[0]):
        totals_ref[plane] = total


def scan_kernel(planes_ref, parts_ref, prefix_ref):
    place = lax.axis_index(BITS["y"])
    running = jnp.zeros_like(planes_ref[0])
    for plane in range(planes_ref.shape[0] - 1):
        running = running + jnp.where(plane < place, planes_ref[index_in(ROWS, y=plane)], 0.0)
    for x, core, z in itertools.product(*(range(size) for size in SIZES[1:])):
        block = index_in(PLANE, x=x, core=core, z=z)
        prefix_ref[block] = running
        running = running + parts_ref[block]


def attend_kernel(
    queries_ref,
    keys_ref,
    values_ref,
    gain_ref,
    prefix_ref,
    inner_ref,
    features_ref,
    out_hbm,
    out_ref,
    left,
):
    def store(first):
        done = pl.ds(first * DK, TOGETHER * DK)
        return pltpu.make_async_copy(
            out_ref.at[:, done], out_hbm.at[:, done], left.at[first // TOGETHER]
        )

    @pl.when(waits_first())
    def _():
        for first in range(0, H, TOGETHER):
            for head in range(first, first + TOGETHER):
                lanes = lanes_of(head)
                fq = features_ref[:, lanes]
                outer = jnp.dot(
                    jnp.concatenate([fq] * 3, axis=1),
                    jnp.concatenate(in_three(prefix_ref[head]), axis=0),
                    preferred_element_type=jnp.float32,
                )
                out_ref[:, lanes] = normed(inner_ref[:, lanes] + outer, gain_ref[:, lanes])
            store(first).start()

    @pl.when(jnp.logical_not(waits_first()))
    def _():
        causal = mask_of(queries_ref.shape[0])
        for first in range(0, H, TOGETHER):
            heads = range(first, first + TOGETHER)
            fq = [feature(queries_ref[:, lanes_of(head)]) for head in heads]
            fk = [feature(keys_ref[:, lanes_of(head)]) for head in heads]
            weights = [scores_of(a, b, causal) for a, b in zip(fq, fk)]
            mixed = []
            for head, a, w in zip(heads, fq, weights):
                right = [values_ref[:, lanes_of(head)], *in_three(prefix_ref[head])]
                mixed.append(
                    jnp.dot(
                        jnp.concatenate([w, a, a, a], axis=1),
                        jnp.concatenate(right, axis=0),
                        preferred_element_type=jnp.float32,
                    )
                )
            for head, part in zip(heads, mixed):
                out_ref[:, lanes_of(head)] = normed(part, gain_ref[:, lanes_of(head)])
            store(first).start()

    for first in range(0, H, TOGETHER):
        store(first).wait()


def on_chip(kernel, count, *results, flops=0):
    whole = pl.BlockSpec(memory_space=pltpu.VMEM)
    shapes = [jax.ShapeDtypeStruct(shape, dtype) for shape, dtype in results]
    return pl.pallas_call(
        kernel,
        out_shape=shapes,
        in_specs=[whole] * count,
        out_specs=[whole] * len(shapes),
        compiler_params=pltpu.CompilerParams(vmem_limit_bytes=12 * 2**20),
        cost_estimate=pl.CostEstimate(
            flops=flops, bytes_accessed=3 * 2**20, transcendentals=0
        ),
    )


def local(queries, keys, values, norm_gain):
    rows, width = queries.shape
    planes, group = SIZES[0], SIZES[1] * SIZES[2] * SIZES[3]
    piece = width // group
    f32 = jnp.float32
    flops = 2 * H * rows * DK * DK
    state, inner, features = pl.pallas_call(
        state_kernel,
        out_shape=[
            jax.ShapeDtypeStruct((H, DK, DK), f32),
            jax.ShapeDtypeStruct((rows, width), f32),
            jax.ShapeDtypeStruct((rows, width), jnp.bfloat16),
        ],
        in_specs=[pl.BlockSpec(memory_space=pl.ANY)] * 3,
        out_specs=[pl.BlockSpec(memory_space=pltpu.VMEM)] * 3,
        scratch_shapes=[pltpu.VMEM((rows, width), jnp.bfloat16)] * 3
        + [pltpu.SemaphoreType.DMA((3, 2))],
        compiler_params=pltpu.CompilerParams(vmem_limit_bytes=LIMIT),
    )(*(pltpu.with_memory_space_constraint(part, pltpu.HBM) for part in (keys, values, queries)))
    parts = lax.all_to_all(state.reshape(group, piece, DK), PLANE, 0, 0, tiled=True)
    [totals] = on_chip(total_kernel, 1, ((planes, piece, DK), f32))(parts)
    totals = lax.all_to_all(totals, ROWS, 0, 0, tiled=True)
    [prefix] = on_chip(scan_kernel, 2, (parts.shape, f32))(totals, parts)
    prefix = lax.all_to_all(prefix, PLANE, 0, 0, tiled=True).reshape(H, DK, DK)
    return pl.pallas_call(
        attend_kernel,
        out_shape=jax.ShapeDtypeStruct((rows, width), jnp.bfloat16),
        in_specs=[pl.BlockSpec(memory_space=pltpu.VMEM)] * 7,
        out_specs=pl.BlockSpec(memory_space=pl.ANY),
        scratch_shapes=[
            pltpu.VMEM((rows, width), jnp.bfloat16),
            pltpu.SemaphoreType.DMA((H // TOGETHER,)),
        ],
        compiler_params=pltpu.CompilerParams(vmem_limit_bytes=LIMIT),
    )(queries, keys, values, norm_gain.reshape(1, width), prefix, inner, features)


def solution(mesh):
    mesh = Mesh(mesh.devices.reshape((2,) * len(WHOLE)), WHOLE)
    split = P(WHOLE, None)
    return jax.shard_map(
        local, mesh=mesh, in_specs=(split, split, split, P()), out_specs=split, check_vma=False
    )
```

```python
import itertools

import jax
import jax.numpy as jnp
from jax import lax
from jax.experimental import pallas as pl
from jax.experimental.pallas import tpu as pltpu
from jax.sharding import Mesh, PartitionSpec as P

H = 16
DK = 128
SIZES = (8, 4, 2, 8)
BITS = {"y": ("y2", "y1", "y0"), "x": ("x1", "x0"), "core": ("core",), "z": ("z2", "z1", "z0")}
WHOLE = tuple(bit for axis in BITS.values() for bit in axis)
ROWS = ("y0", "y1", "y2")
PLANE = ("z2", "z1", "z0", "core", "x1", "x0")


def index_in(order, **place):
    index = 0
    for bit in order:
        axis = bit.rstrip("012")
        index = 2 * index + (place[axis] >> int(bit[len(axis) :] or 0)) % 2
    return index


TOGETHER = 4
LIMIT = 16 * 2**20


def feature(rows):
    wide = rows.astype(jnp.float32)
    grown = jnp.where(wide > 0.0, wide + 1.0, jnp.exp(jnp.minimum(wide, 0.0)))
    return grown.astype(jnp.bfloat16)


def lanes_of(head):
    return slice(head * DK, (head + 1) * DK)


def scores_of(fq, fk, causal):
    scores = lax.dot_general(
        fq, fk, (((1,), (1,)), ((), ())), preferred_element_type=jnp.float32
    )
    return jnp.where(causal, scores, 0.0).astype(jnp.bfloat16)


def mask_of(rows):
    at = lax.broadcasted_iota(jnp.int32, (rows, rows), 0)
    return lax.broadcasted_iota(jnp.int32, (rows, rows), 1) <= at


def in_three(prefix):
    high = prefix.astype(jnp.bfloat16)
    rest = prefix - high.astype(jnp.float32)
    middle = rest.astype(jnp.bfloat16)
    return [high, middle, (rest - middle.astype(jnp.float32)).astype(jnp.bfloat16)]


def normed(mixed, gain):
    meansq = jnp.mean(mixed * mixed, axis=-1, keepdims=True)
    return (gain * mixed * lax.rsqrt(meansq + 1e-05)).astype(jnp.bfloat16)


def waits_first():
    return lax.axis_index(BITS["z"]) < SIZES[3] // 2


def state_kernel(
    keys_hbm,
    values_hbm,
    queries_hbm,
    state_ref,
    inner_ref,
    features_ref,
    keys_ref,
    values_ref,
    queries_ref,
    arrived,
):
    def load(number, half):
        source, target = (
            (keys_hbm, keys_ref),
            (values_hbm, values_ref),
            (queries_hbm, queries_ref),
        )[number]
        rows = pl.ds(half * (target.shape[0] // 2), target.shape[0] // 2)
        return pltpu.make_async_copy(
            source.at[rows], target.at[rows], arrived.at[number, half]
        )

    for half in range(2):
        for number in range(2):
            load(number, half).start()
    for half in range(2):
        rows = slice(half * (keys_ref.shape[0] // 2), (half + 1) * (keys_ref.shape[0] // 2))
        for number in range(2):
            load(number, half).wait()
        for head in range(H):
            part = lax.dot_general(
                feature(keys_ref[rows, lanes_of(head)]),
                values_ref[rows, lanes_of(head)],
                (((0,), (0,)), ((), ())),
                preferred_element_type=jnp.float32,
            )
            state_ref[head] = part if half == 0 else state_ref[head] + part

    @pl.when(waits_first())
    def _():
        for half in range(2):
            load(2, half).start()
        for half in range(2):
            load(2, half).wait()
        causal = mask_of(queries_ref.shape[0])
        for first in range(0, H, TOGETHER):
            lanes = [lanes_of(head) for head in range(first, first + TOGETHER)]
            fq = [feature(queries_ref[:, part]) for part in lanes]
            fk = [feature(keys_ref[:, part]) for part in lanes]
            weights = [scores_of(a, b, causal) for a, b in zip(fq, fk)]
            for part, a, w in zip(lanes, fq, weights):
                inner_ref[:, part] = jnp.dot(
                    w, values_ref[:, part], preferred_element_type=jnp.float32
                )
                features_ref[:, part] = a


def total_kernel(parts_ref, totals_ref):
    sums = [parts_ref[lane] for lane in range(4)]
    for block in range(4, parts_ref.shape[0]):
        sums[block % 4] = sums[block % 4] + parts_ref[block]
    total = (sums[0] + sums[1]) + (sums[2] + sums[3])
    for plane in range(totals_ref.shape[0]):
        totals_ref[plane] = total


def scan_kernel(planes_ref, parts_ref, prefix_ref):
    place = lax.axis_index(BITS["y"])
    running = jnp.zeros_like(planes_ref[0])
    for plane in range(planes_ref.shape[0] - 1):
        running = running + jnp.where(plane < place, planes_ref[index_in(ROWS, y=plane)], 0.0)
    for x, core, z in itertools.product(*(range(size) for size in SIZES[1:])):
        block = index_in(PLANE, x=x, core=core, z=z)
        prefix_ref[block] = running
        running = running + parts_ref[block]


def attend_kernel(
    queries_ref,
    keys_ref,
    values_ref,
    gain_ref,
    prefix_ref,
    inner_ref,
    features_ref,
    out_hbm,
    out_ref,
    left,
):
    def store(first):
        done = pl.ds(first * DK, TOGETHER * DK)
        return pltpu.make_async_copy(
            out_ref.at[:, done], out_hbm.at[:, done], left.at[first // TOGETHER]
        )

    @pl.when(waits_first())
    def _():
        for first in range(0, H, TOGETHER):
            for head in range(first, first + TOGETHER):
                lanes = lanes_of(head)
                fq = features_ref[:, lanes]
                outer = jnp.dot(
                    jnp.concatenate([fq] * 3, axis=1),
                    jnp.concatenate(in_three(prefix_ref[head]), axis=0),
                    preferred_element_type=jnp.float32,
                )
                out_ref[:, lanes] = normed(inner_ref[:, lanes] + outer, gain_ref[:, lanes])
            store(first).start()

    @pl.when(jnp.logical_not(waits_first()))
    def _():
        causal = mask_of(queries_ref.shape[0])
        for first in range(0, H, TOGETHER):
            heads = range(first, first + TOGETHER)
            fq = [feature(queries_ref[:, lanes_of(head)]) for head in heads]
            fk = [feature(keys_ref[:, lanes_of(head)]) for head in heads]
            weights = [scores_of(a, b, causal) for a, b in zip(fq, fk)]
            mixed = []
            for head, a, w in zip(heads, fq, weights):
                right = [values_ref[:, lanes_of(head)], *in_three(prefix_ref[head])]
                mixed.append(
                    jnp.dot(
                        jnp.concatenate([w, a, a, a], axis=1),
                        jnp.concatenate(right, axis=0),
                        preferred_element_type=jnp.float32,
                    )
                )
            for head, part in zip(heads, mixed):
                out_ref[:, lanes_of(head)] = normed(part, gain_ref[:, lanes_of(head)])
            store(first).start()

    for first in range(0, H, TOGETHER):
        store(first).wait()


def on_chip(kernel, count, *results, flops=0):
    whole = pl.BlockSpec(memory_space=pltpu.VMEM)
    shapes = [jax.ShapeDtypeStruct(shape, dtype) for shape, dtype in results]
    return pl.pallas_call(
        kernel,
        out_shape=shapes,
        in_specs=[whole] * count,
        out_specs=[whole] * len(shapes),
        compiler_params=pltpu.CompilerParams(vmem_limit_bytes=12 * 2**20),
        cost_estimate=pl.CostEstimate(
            flops=flops, bytes_accessed=3 * 2**20, transcendentals=0
        ),
    )


def local(queries, keys, values, norm_gain):
    rows, width = queries.shape
    planes, group = SIZES[0], SIZES[1] * SIZES[2] * SIZES[3]
    piece = width // group
    f32 = jnp.float32
    flops = 2 * H * rows * DK * DK
    state, inner, features = pl.pallas_call(
        state_kernel,
        out_shape=[
            jax.ShapeDtypeStruct((H, DK, DK), f32),
            jax.ShapeDtypeStruct((rows, width), f32),
            jax.ShapeDtypeStruct((rows, width), jnp.bfloat16),
        ],
        in_specs=[pl.BlockSpec(memory_space=pl.ANY)] * 3,
        out_specs=[pl.BlockSpec(memory_space=pltpu.VMEM)] * 3,
        scratch_shapes=[pltpu.VMEM((rows, width), jnp.bfloat16)] * 3
        + [pltpu.SemaphoreType.DMA((3, 2))],
        compiler_params=pltpu.CompilerParams(vmem_limit_bytes=LIMIT),
    )(*(pltpu.with_memory_space_constraint(part, pltpu.HBM) for part in (keys, values, queries)))
    parts = lax.all_to_all(state.reshape(group, piece, DK), PLANE, 0, 0, tiled=True)
    [totals] = on_chip(total_kernel, 1, ((planes, piece, DK), f32))(parts)
    totals = lax.all_to_all(totals, ROWS, 0, 0, tiled=True)
    [prefix] = on_chip(scan_kernel, 2, (parts.shape, f32))(totals, parts)
    prefix = lax.all_to_all(prefix, PLANE, 0, 0, tiled=True).reshape(H, DK, DK)
    return pl.pallas_call(
        attend_kernel,
        out_shape=jax.ShapeDtypeStruct((rows, width), jnp.bfloat16),
        in_specs=[pl.BlockSpec(memory_space=pltpu.VMEM)] * 7,
        out_specs=pl.BlockSpec(memory_space=pl.ANY),
        scratch_shapes=[
            pltpu.VMEM((rows, width), jnp.bfloat16),
            pltpu.SemaphoreType.DMA((H // TOGETHER,)),
        ],
        compiler_params=pltpu.CompilerParams(vmem_limit_bytes=LIMIT),
    )(queries, keys, values, norm_gain.reshape(1, width), prefix, inner, features)


def solution(mesh):
    mesh = Mesh(mesh.devices.reshape((2,) * len(WHOLE)), WHOLE)
    split = P(WHOLE, None)
    return jax.shard_map(
        local, mesh=mesh, in_specs=(split, split, split, P()), out_specs=split, check_vma=False
    )
```
